32 devices in a mesh: runs: 2 (over x), az: 16 (over z, y, core).
Axes of the slice: x: 2, y: 2, z: 4, core: 2. Of those that a mesh axis runs over, the one named last changes fastest.
Arguments:
- state: float32 [8, 4, 32, 2048], P(None, 'runs', None, 'az'), parts along dimension 1, may hold values from -6 to 6
- offsets: int32 [80], P('runs'), parts along dimension 0, may hold values from 0 to 2047, as said below
- fraction: float32 [80], P('runs'), parts along dimension 0, may hold values from 0 to 1, as said below
- speeds: float32 [3, 8], replicated, may hold values from -1 to 1
- coupling: float32 [8, 8], replicated, may hold values from -2 to 2
Outputs:
- advanced: float32 [8, 4, 32, 2048], P(None, 'runs', None, 'az'), parts along dimension 1
The draws below stay inside these ranges and needn't reach their ends.
There are 2 independent parts, one for each index of `runs`. The reference program is written for one: setup_inputs(seed, part) draws one part's arguments, and reference() takes and returns one part's arrays. A program takes and returns all parts, laid end to end along the dimension named above; an argument that names none is the same for every part. Nothing has to cross between parts.
Inputs may be any that keep to these rules, and one draw needn't show every extreme that they name: offsets + fraction is one orbital offset that rises along the rows by 128 / 9 cells a row, modulo 2048; offsets is its whole part. At most 9 of the 40 rows share one value of offsets // 128, and exactly 9 rows share one value. `fraction`: the fractional part of the same orbital offset whose whole part is offsets.
All inputs are finite; a program needn't handle non-finite values.
Results may differ from the reference program's by a relative error of at most 0.0003.
Values sent between devices are 32-bit elements; how exact they have to be, the bound alone decides.
No kernel may reach another device: no remote copies, remote signals or barrier semaphores. Data moves between devices by JAX's collectives and lax.ppermute only.
A program may use at most 64 MiB of HBM per device.

```python
import jax
import jax.numpy as jnp
from jax import lax

FIELDS = 8
NX = 32
NZ = 2
AZ_DEV = 128
NY = 2048
CAP = 9


def ramp_values(key):
    total_rows = NX + 8
    phase = jax.random.randint(key, (), 0, NY * CAP)
    scaled = phase + jnp.arange(total_rows, dtype=jnp.int32) * AZ_DEV
    whole = scaled // CAP % NY
    leftover = scaled % CAP
    return (whole.astype(jnp.int32), leftover)


def draw_offsets(key, part):
    whole, leftover = ramp_values(key)
    return whole


def draw_fraction(key, part):
    whole, leftover = ramp_values(key)
    key = jax.random.fold_in(key, 11)
    extra = jax.random.uniform(key, (), jnp.float32, 0.0, 0.999)
    return (leftover.astype(jnp.float32) + extra) / CAP


def level_of(stream_key, extent, pieces, smallest, top_value):
    loudness = 1.0
    for axis_at, parts in pieces:
        steps = jax.random.uniform(jax.random.fold_in(jax.random.fold_in(stream_key, 6), axis_at), (parts,), jnp.float32, smallest / len(pieces), top_value / len(pieces))
        loudness = loudness * jnp.repeat(jnp.exp(steps), extent[axis_at] // parts).reshape((-1,) + (1,) * (len(extent) - 1 - axis_at))
    return loudness


def normal_values(own_key, extent, width, limit, cuts=(), kind=jnp.bfloat16):
    level = level_of(own_key, extent, cuts, -0.22, 0.18) if cuts else 1.0
    entries = jax.random.normal(own_key, extent, jnp.float32) * width * level
    return jnp.minimum(jnp.maximum(entries, -limit), limit).astype(kind)


def setup_inputs(seed: int = 0, part: int = 0) -> dict:
    splits = jax.random.split(jax.random.key(seed), 6)
    part_splits = jax.random.split(jax.random.fold_in(splits[5], part), 6)
    return {
        "state": normal_values(part_splits[0], (FIELDS, NZ, NX, NY), 1.0, 6.0, ((3, 16),), jnp.float32),
        "offsets": draw_offsets(jax.random.fold_in(jax.random.fold_in(splits[5], part), 71), part),
        "fraction": draw_fraction(jax.random.fold_in(jax.random.fold_in(splits[5], part), 71), part),
        "speeds": jnp.clip(jax.random.uniform(splits[3], (3, FIELDS), jnp.float32, -1.0, 1.0), -1.0, 1.0),
        "coupling": normal_values(splits[4], (FIELDS, FIELDS), FIELDS ** -0.5, 2.0, (), jnp.float32),
    }


courant = 0.3


def minmod_slope(lower, upper):
    return 0.5 * (jnp.sign(lower) + jnp.sign(upper)) * jnp.minimum(jnp.abs(lower), jnp.abs(upper))


def face_update(field, speed, axis):
    length = field.shape[axis]
    jumps = lax.slice_in_dim(field, 1, length, axis=axis) - lax.slice_in_dim(field, 0, length - 1, axis=axis)
    slope = minmod_slope(lax.slice_in_dim(jumps, 0, length - 2, axis=axis), lax.slice_in_dim(jumps, 1, length - 1, axis=axis))
    cells = lax.slice_in_dim(field, 1, length - 1, axis=axis)
    left_state = lax.slice_in_dim(cells, 0, length - 3, axis=axis) + 0.5 * (1.0 - courant * speed) * lax.slice_in_dim(slope, 0, length - 3, axis=axis)
    right_state = lax.slice_in_dim(cells, 1, length - 2, axis=axis) - 0.5 * (1.0 + courant * speed) * lax.slice_in_dim(slope, 1, length - 2, axis=axis)
    flux = speed * jnp.where(speed > 0.0, left_state, right_state)
    return lax.slice_in_dim(flux, 1, length - 3, axis=axis) - lax.slice_in_dim(flux, 0, length - 4, axis=axis)


def advance(field, speeds, coupling):
    core = field[:, :, 2:-2, 2:-2]
    wrapped = jnp.concatenate([core[:, -2:], core, core[:, :2]], axis=1)
    speed_x = speeds[0].reshape(-1, 1, 1, 1)
    speed_y = speeds[1].reshape(-1, 1, 1, 1)
    speed_z = speeds[2].reshape(-1, 1, 1, 1)
    along_x = face_update(field[:, :, :, 2:-2], speed_x, 2)
    along_y = face_update(field[:, :, 2:-2, :], speed_y, 3)
    along_z = face_update(wrapped, speed_z, 1)
    mixing = jnp.einsum("fg,gzxy->fzxy", coupling, core, precision=lax.Precision.HIGHEST)
    return core - courant * (along_x + along_y + along_z) + courant * mixing


def reference(state, offsets, fraction, speeds, coupling):
    rows = state.shape[2]
    cols = state.shape[3]
    extended = jnp.concatenate([state[:, :, rows - 4:], state, state[:, :, :4]], axis=2)
    column = jnp.arange(cols, dtype=jnp.int32)
    source = (column[None, :] - offsets.astype(jnp.int32)[:, None]) % cols
    before = (source - 1) % cols
    full_shape = extended.shape
    upper = jnp.take_along_axis(extended, jnp.broadcast_to(source[None, None], full_shape), axis=3)
    lower = jnp.take_along_axis(extended, jnp.broadcast_to(before[None, None], full_shape), axis=3)
    weight = fraction[None, None, :, None]
    shifted = (1.0 - weight) * upper + weight * lower
    padded = jnp.concatenate([shifted[..., cols - 4:], shifted, shifted[..., :4]], axis=3)
    first = advance(padded, speeds, coupling)
    return 0.5 * (padded[:, :, 4:-4, 4:-4] + advance(first, speeds, coupling))
```

```python
import functools

import jax
import jax.numpy as jnp
from jax import lax
from jax.experimental import pallas as pl
from jax.experimental.pallas import tpu as pltpu
from jax.sharding import PartitionSpec as P

courant = 0.3
GHOST = 4
EDGE = 2 * GHOST + 1
STRIP = 4 * GHOST


def rows_per_block(devices):
    return 9 if devices <= 16 else 6


class Shifts:
    def __init__(self, offs, cap, span, cells):
        self.offs, self.span, self.cells = offs, span, cells
        self.start = self.within(0)
        late = [(self.within(m) < self.start).astype(jnp.int32) for m in range(1, cap)]
        self.base = functools.reduce(lambda a, b: a + b, late) + 1

    def within(self, x):
        return (self.offs[x] + (self.span - GHOST)) & (self.span - 1)

    def group(self, x):
        return ((self.offs[x] - self.offs[0] + self.start) & (self.cells - 1)) >> (
            self.span.bit_length() - 1
        )


def pack_kernel(cap, nx, planes, cells, offs, state, packed, rolled):
    nfields, span = packed.shape[2:]
    total = nx + 2 * GHOST
    groups = packed.shape[0] // (cap + 1)
    shifts = Shifts(offs, cap, span, cells)
    tile = (nfields, span)
    lane = lax.broadcasted_iota(jnp.int32, tile, 1)

    def one_row(x, m):
        within, group = shifts.within(x), shifts.group(x)
        source = jnp.where(x < GHOST, x + nx - GHOST, jnp.where(x >= nx + GHOST, x - nx - GHOST, x - GHOST))
        near = lane >= within
        offset = lane - EDGE * m
        member = (offset >= 0) & (offset < EDGE)
        nearer = offset + (span - EDGE) >= within
        at = x + group + shifts.base
        ext = (cap + 1) * (group + 1)
        for z in range(planes):
            rows = state[pl.ds(source + z * nx, nfields, stride=planes * nx), :]
            value = pltpu.roll(rows, within, 1)
            rolled[x + cap, z] = value
            packed[at, z] = jnp.where(near, value, rolled[x, z])
            piece = pltpu.roll(value, EDGE * (m + 1), 1)
            packed[ext, z] = jnp.where(member & nearer, piece, packed[ext, z])

            @pl.when((within > span - EDGE) & (group + 2 < groups))
            def _():
                far = ext + (cap + 1)
                packed[far, z] = jnp.where(member & ~nearer, piece, packed[far, z])

    def some_rows(i, m):
        for u in range(4):
            one_row(4 * i + u, m)
            m = jnp.where(m == cap - 1, 0, m + 1)
        return m

    lax.fori_loop(0, total // 4, some_rows, jnp.int32(0))

    def tail_row(x, carry):
        at = x + shifts.group(x) + shifts.base + cap + 1
        for z in range(planes):
            packed[at, z] = rolled[x + cap, z]
        return carry

    lax.fori_loop(total - cap, total, tail_row, 0)


def minmod(lower, upper):
    return jnp.maximum(jnp.minimum(upper, 0.0), jnp.minimum(lower, jnp.maximum(upper, 0.0)))


def step_kernel(cap, nx, planes, cells, messages, offs, frac, speeds, coupling, *refs):
    arrived = refs[: len(messages)]
    out, packed, shifted, first, second, sem = refs[len(messages) :]
    nfields, span = packed.shape[2:]
    total = nx + 2 * GHOST
    groups = packed.shape[0] // (cap + 1)
    tile = (nfields, span)
    copies = []
    for j, (at, size) in enumerate(messages):
        copies.append(pltpu.make_async_copy(arrived[j], packed.at[pl.ds(at, size)], sem.at[j]))
        copies[-1].start()

    shifts = Shifts(offs, cap, span, cells)
    lane = lax.broadcasted_iota(jnp.int32, tile, 1)
    slot = lane // STRIP
    lower_half = lane < span // 2
    first_lane = lane == 0
    count = total * STRIP // span
    wide = count + 4

    def column(values):
        picked = jnp.where(
            lax.broadcasted_iota(jnp.int32, (nfields, nfields), 0)
            == lax.broadcasted_iota(jnp.int32, (nfields, nfields), 1),
            values,
            0.0,
        )
        return jnp.broadcast_to(jnp.sum(picked, axis=1, keepdims=True), tile)

    flux = []
    for axis in range(3):
        speed = column(speeds[axis : axis + 1, :])
        positive = speed > 0.0
        slope_part = jnp.where(
            positive, 0.5 * (1.0 - courant * speed), -0.5 * (1.0 + courant * speed)
        )
        scaled = -courant * speed
        flux.append((scaled, scaled * slope_part, positive))
    mix = []
    rows = lax.broadcasted_iota(jnp.int32, (nfields, nfields), 0)
    cols = lax.broadcasted_iota(jnp.int32, (nfields, nfields), 1)
    for r in range(nfields):
        picked = jnp.where((rows - cols) % nfields == r, coupling[...], 0.0)
        mix.append(jnp.broadcast_to(courant * jnp.sum(picked, axis=1, keepdims=True), tile))
    mix[0] = mix[0] + 1.0
    (sx, tx, px), (sy, ty, py), (sz, tz, pz) = flux

    for copy in copies:
        copy.wait()

    def remap_row(x, m, g, i):
        within, group = shifts.within(x), shifts.group(x)
        near = lane >= within
        nearer = lane >= within + (EDGE * (m + 1) - span)
        at = x + group + shifts.base
        ext = (cap + 1) * (group + 1)
        far = (cap + 1) * jnp.minimum(group + 2, groups - 1)
        f = frac[x]
        for z in range(planes):
            upper = jnp.where(near, packed[at, z], packed[at + (cap + 1), z])
            edge = pltpu.roll(
                jnp.where(nearer, packed[ext, z], packed[far, z]), span - EDGE * (m + 1), 1
            )
            edge_lower = pltpu.roll(edge, 1, 1)
            lower = jnp.where(first_lane, edge_lower, pltpu.roll(upper, 1, 1))
            body = (1.0 - f) * upper + f * lower
            edge = (1.0 - f) * edge + f * edge_lower
            shifted[wide + x, z] = body
            piece = pltpu.roll(
                jnp.where(lower_half, body, edge), (STRIP * g + STRIP // 2) & (span - 1), 1
            )
            shifted[2 + i, z] = jnp.where(slot == g, piece, shifted[2 + i, z])

    def remap_rows(g, m):
        for i in range(count):
            remap_row(count * g + i, m, g, i)
            m = jnp.where(m == cap - 1, 0, m + 1)
        return m

    lax.fori_loop(0, total // count, remap_rows, jnp.int32(0))

    def wrap_strips(ref):
        for z in range(planes):
            for i in range(2):
                ref[i, z] = pltpu.roll(ref[i + count, z], STRIP, 1)
                ref[2 + count + i, z] = pltpu.roll(ref[2 + i, z], span - STRIP, 1)

    def state_of(u, before, after):
        return sx * u + tx * minmod(before, after)

    def advance(source, unroll, steps, emit):
        def enter(z):
            u = [source[i, z] for i in range(4)]
            jumps = [u[i + 1] - u[i] for i in range(3)]
            low = state_of(u[1], jumps[0], jumps[1])
            here = state_of(u[2], jumps[1], jumps[2])
            return u[2], u[3], jumps[2], here, here - low

        def body(step, carry):
            for k in range(unroll):
                x = 2 + step * unroll + k
                vertical = []
                for z in range(planes):
                    u = carry[z][0]
                    above, below = carry[(z + 1) % planes][0], carry[(z - 1) % planes][0]
                    vertical.append(sz * u + tz * minmod(u - below, above - u))
                following = []
                for z in range(planes):
                    u, ahead_u, jump, here, behind_face = carry[z]
                    beyond = source[x + 2, z]
                    next_jump = beyond - ahead_u
                    there = state_of(ahead_u, jump, next_jump)
                    face = there - here
                    following.append((ahead_u, beyond, next_jump, there, face))
                    value = mix[0] * u + jnp.where(px, behind_face, face)
                    for r in range(1, nfields):
                        value = value + mix[r] * pltpu.roll(u, r, 0)
                    value = value + jnp.where(
                        pz,
                        vertical[z] - vertical[(z - 1) % planes],
                        vertical[(z + 1) % planes] - vertical[z],
                    )
                    ahead = pltpu.roll(u, span - 1, 1) - u
                    along = sy * u + ty * minmod(pltpu.roll(ahead, 1, 1), ahead)
                    side = pltpu.roll(along, span - 1, 1) - along
                    emit(x - 2, z, value + jnp.where(py, pltpu.roll(side, 1, 1), side))
                carry = tuple(following)
            return carry

        lax.fori_loop(0, steps, body, tuple(enter(z) for z in range(planes)))

    def put_first(x, z, value):
        first[x + 2, z] = value

    def put_second(x, z, value):
        second[x, z] = value

    wrap_strips(shifted)
    advance(shifted, 5, (total + wide - 4) // 5, put_first)
    wrap_strips(first)
    advance(first, 5, (total + wide - 4) // 5, put_second)

    begins = lane < STRIP // 2

    def put_row(g, i, row):
        turn = (span - STRIP * g - GHOST) & (span - 1)
        for z in range(planes):
            head = pltpu.roll(shifted[2 + i, z] + second[i, z], turn, 1)
            body = pltpu.roll(shifted[wide + row, z] + second[wide - 2 + row, z], GHOST, 1)
            out[pl.ds(row - GHOST + z * nx, nfields, stride=planes * nx), :] = 0.5 * jnp.where(
                begins, head, body
            )

    def put_rows(step, carry):
        for k in range(4):
            row = GHOST + 4 * step + k
            g = (row * (65536 // count + 1)) >> 16
            put_row(g, row - count * g, row)
        return carry

    lax.fori_loop(0, nx // 4, put_rows, 0)


def per_device(state, offsets, fraction, speeds, coupling):
    nfields, planes, nx, span = state.shape
    devices = lax.axis_size("az")
    cells = devices * span
    cap = rows_per_block(devices)
    total = nx + 2 * GHOST
    few = total % cap
    groups = total // cap + 3
    unit = cap + 1
    vmem = pl.BlockSpec(memory_space=pltpu.VMEM)
    smem = pl.BlockSpec(memory_space=pltpu.SMEM)
    hbm = pl.BlockSpec(memory_space=pl.ANY)
    packed = pl.pallas_call(
        functools.partial(pack_kernel, cap, nx, planes, cells),
        out_shape=jax.ShapeDtypeStruct((unit * groups, planes, nfields, span), jnp.float32),
        in_specs=[smem, vmem],
        out_specs=vmem,
        scratch_shapes=[pltpu.VMEM((total + cap, planes, nfields, span), jnp.float32)],
        name="pack",
    )(offsets, state.reshape(nfields * planes * nx, span))

    messages = [(1, cap)] + [(unit * j, unit) for j in range(1, groups - 1)] + [(unit * (groups - 1), few)]

    def branch(block, count):
        def send(buffer):
            received = []
            for j, (at, size) in enumerate(messages):
                part = lax.slice_in_dim(buffer, at, at + size, axis=0)
                steps = (block + j) % devices
                if steps and j < count:
                    part = lax.ppermute(
                        part, "az", [(i, (i + steps) % devices) for i in range(devices)]
                    )
                received.append(part)
            return received

        return send

    branches = [branch(block, count) for block in range(devices) for count in (groups - 1, groups)]
    begin = offsets[0] + (cells - GHOST)
    block = (begin // span) % devices
    within = begin % span
    last = (offsets[few] + (cells - GHOST)) % span
    which = 2 * block + (last < within).astype(jnp.int32)
    arrived = lax.switch(which, branches, packed)

    wide = total * STRIP // span + 4
    rows = [unit * groups, wide + total, wide + total, wide + total - 4]
    out = pl.pallas_call(
        functools.partial(step_kernel, cap, nx, planes, cells, messages),
        out_shape=jax.ShapeDtypeStruct((nfields * planes * nx, span), jnp.float32),
        in_specs=[smem, smem, vmem, vmem] + [hbm] * groups,
        out_specs=vmem,
        scratch_shapes=[pltpu.VMEM((r, planes, nfields, span), jnp.float32) for r in rows]
        + [pltpu.SemaphoreType.DMA((groups,))],
        name="step",
    )(offsets, fraction, speeds, coupling, *arrived)
    return out.reshape(state.shape)


def solution(mesh):
    return jax.shard_map(
        per_device,
        mesh=mesh,
        in_specs=(P(None, "runs", None, "az"), P("runs"), P("runs"), P(), P()),
        out_specs=P(None, "runs", None, "az"),
        check_vma=False,
    )
```

```python
import functools

import jax
import jax.numpy as jnp
from jax import lax
from jax.experimental import pallas as pl
from jax.experimental.pallas import tpu as pltpu
from jax.sharding import PartitionSpec as P

courant = 0.3
GHOST = 4
EDGE = 2 * GHOST + 1
STRIP = 4 * GHOST


def rows_per_block(devices):
    return 9 if devices <= 16 else 6


class Shifts:
    def __init__(self, offs, cap, span):
        self.offs, self.cap, self.span = offs, cap, span
        start = self.within(0)
        late = [(self.within(m) < start).astype(jnp.int32) for m in range(1, cap)]
        self.base = functools.reduce(lambda a, b: a + b, late) + 1

    def within(self, x):
        return (self.offs[x] + (self.span - GHOST)) & (self.span - 1)

    def of_slot(self, i):
        return self.within(jnp.where(i < self.base, i + self.cap, i) - self.base)


def pack_kernel(cap, nx, planes, devices, offs, state, *refs):
    sent, key = refs[:-1], refs[-1]
    nfields, span = sent[0].shape[2:]
    total = nx + 2 * GHOST
    groups = len(sent)
    shifts = Shifts(offs, cap, span)
    few = sent[-1].shape[0]
    block = ((offs[0] + (devices * span - GHOST)) >> (span.bit_length() - 1)) & (devices - 1)
    key[0] = 2 * block + (shifts.base >= cap + 1 - few).astype(jnp.int32)
    tile = (nfields, span)
    lane = lax.broadcasted_iota(jnp.int32, tile, 1)

    def row(i, k, z, within):
        x = cap * k + i - shifts.base
        source = jnp.where(x < GHOST, x + nx, x) - GHOST
        source = jnp.where(source >= nx, source - nx, source)
        rows = state[pl.ds(jnp.clip(source, 0, nx - 1) + z * nx, nfields, stride=planes * nx), :]
        return pltpu.roll(rows, within, 1)

    def one_slot(i, carry):
        edges, nearer = carry
        within = shifts.of_slot(i)
        near = lane >= within
        offset = lane - EDGE * (i - 1)
        member = (offset >= 0) & (offset < EDGE)
        nearer = jnp.where(member, (offset + (span - EDGE) >= within).astype(jnp.int32), nearer)
        new = []
        for z in range(planes):
            before = None
            for k in range(groups - 1):
                value = row(i, k, z, within)
                merged = value if k == 0 else jnp.where(near, value, before)
                sent[k][i - 1 if k == 0 else i, z] = merged
                piece = pltpu.roll(value, EDGE * i, 1)
                new.append(jnp.where(member, piece, edges[z * (groups - 1) + k]))
                before = value
        return tuple(new), nearer

    def some_slots(step, carry):
        for u in range(3):
            carry = one_slot(3 * step + u + 1, carry)
        return carry

    zero = jnp.zeros(tile, jnp.float32)
    edges, nearer = lax.fori_loop(
        0, cap // 3, some_slots, ((zero,) * (planes * (groups - 1)), jnp.zeros(tile, jnp.int32))
    )
    nearer = nearer > 0
    for z in range(planes):
        for i in range(1, few):
            sent[-1][i, z] = row(i, groups - 2, z, shifts.of_slot(i))
        for j in range(1, groups):
            near_edge = edges[z * (groups - 1) + j - 1]
            far_edge = edges[z * (groups - 1) + max(j - 2, 0)]
            sent[j][0, z] = jnp.where(nearer, near_edge, far_edge)


def minmod(lower, upper):
    return jnp.maximum(jnp.minimum(upper, 0.0), jnp.minimum(lower, jnp.maximum(upper, 0.0)))


def step_kernel(cap, nx, planes, groups, offs, frac, speeds, coupling, *refs):
    arrived = refs[:groups]
    out, shifted, first, second = refs[groups:]
    nfields, span = arrived[0].shape[2:]
    total = nx + 2 * GHOST
    few = arrived[-1].shape[0]
    tile = (nfields, span)
    wide = cap + 5
    shifts = Shifts(offs, cap, span)
    lane = lax.broadcasted_iota(jnp.int32, tile, 1)
    slot = lane // STRIP
    lower_half = lane < span // 2
    first_lane = lane == 0

    def column(values):
        picked = jnp.where(
            lax.broadcasted_iota(jnp.int32, (nfields, nfields), 0)
            == lax.broadcasted_iota(jnp.int32, (nfields, nfields), 1),
            values,
            0.0,
        )
        return jnp.broadcast_to(jnp.sum(picked, axis=1, keepdims=True), tile)

    flux = []
    for axis in range(3):
        speed = column(speeds[axis : axis + 1, :])
        positive = speed > 0.0
        slope_part = jnp.where(
            positive, 0.5 * (1.0 - courant * speed), -0.5 * (1.0 + courant * speed)
        )
        scaled = -courant * speed
        flux.append((scaled, scaled * slope_part, positive))
    mix = []
    rows = lax.broadcasted_iota(jnp.int32, (nfields, nfields), 0)
    cols = lax.broadcasted_iota(jnp.int32, (nfields, nfields), 1)
    for r in range(nfields):
        picked = jnp.where((rows - cols) % nfields == r, coupling[...], 0.0)
        mix.append(jnp.broadcast_to(courant * jnp.sum(picked, axis=1, keepdims=True), tile))
    mix[0] = mix[0] + 1.0
    (sx, tx, px), (sy, ty, py), (sz, tz, pz) = flux

    def remap_slot(i):
        within = shifts.of_slot(i)
        near = lane >= within
        nearer = lane >= within + (EDGE * i - span)
        for z in range(planes):
            strip = None
            for k in range(groups - 1):
                x = jnp.clip(cap * k + i - shifts.base, -1, total)
                f = frac[jnp.clip(x, 0, total - 1)]
                here = arrived[k][i - 1 if k == 0 else i, z]
                after = arrived[k + 1][i if k + 2 < groups else jnp.minimum(i, few - 1), z]
                upper = jnp.where(near, here, after)
                ends = arrived[k + 1][0, z]
                if k + 2 < groups:
                    ends = jnp.where(nearer, ends, arrived[k + 2][0, z])
                edge = pltpu.roll(ends, span - EDGE * i, 1)
                edge_lower = pltpu.roll(ends, span - EDGE * i + 1, 1)
                lower = jnp.where(first_lane, edge_lower, pltpu.roll(upper, 1, 1))
                body = (1.0 - f) * upper + f * lower
                edge = (1.0 - f) * edge + f * edge_lower
                shifted[wide + x, z] = body
                piece = pltpu.roll(
                    jnp.where(lower_half, body, edge), (STRIP * k + STRIP // 2) % span, 1
                )
                strip = piece if k == 0 else jnp.where(slot == k, piece, strip)
            shifted[1 + i, z] = strip

    def remap_slots(step, carry):
        for u in range(3):
            remap_slot(3 * step + u + 1)
        return carry

    lax.fori_loop(0, cap // 3, remap_slots, 0)

    def wrap_strips(ref):
        for z in range(planes):
            for i in range(2):
                ref[i, z] = pltpu.roll(ref[i + cap, z], STRIP, 1)
                ref[2 + cap + i, z] = pltpu.roll(ref[2 + i, z], span - STRIP, 1)

    def state_of(u, before, after):
        return sx * u + tx * minmod(before, after)

    def advance(source, unroll, steps, emit):
        def enter(z):
            u = [source[i, z] for i in range(4)]
            jumps = [u[i + 1] - u[i] for i in range(3)]
            low = state_of(u[1], jumps[0], jumps[1])
            here = state_of(u[2], jumps[1], jumps[2])
            return u[2], u[3], jumps[2], here, here - low

        def body(step, carry):
            for k in range(unroll):
                x = 2 + step * unroll + k
                vertical = []
                for z in range(planes):
                    u = carry[z][0]
                    above, below = carry[(z + 1) % planes][0], carry[(z - 1) % planes][0]
                    vertical.append(sz * u + tz * minmod(u - below, above - u))
                following = []
                for z in range(planes):
                    u, ahead_u, jump, here, behind_face = carry[z]
                    beyond = source[x + 2, z]
                    next_jump = beyond - ahead_u
                    there = state_of(ahead_u, jump, next_jump)
                    face = there - here
                    following.append((ahead_u, beyond, next_jump, there, face))
                    value = mix[0] * u + jnp.where(px, behind_face, face)
                    for r in range(1, nfields):
                        value = value + mix[r] * pltpu.roll(u, r, 0)
                    value = value + jnp.where(
                        pz,
                        vertical[z] - vertical[(z - 1) % planes],
                        vertical[(z + 1) % planes] - vertical[z],
                    )
                    along = sy * u + ty * minmod(
                        u - pltpu.roll(u, 1, 1), pltpu.roll(u, span - 1, 1) - u
                    )
                    side = jnp.where(
                        py, along - pltpu.roll(along, 1, 1), pltpu.roll(along, span - 1, 1) - along
                    )
                    emit(x, z, value + side)
                carry = tuple(following)
            return carry

        lax.fori_loop(0, steps, body, tuple(enter(z) for z in range(planes)))

    def put_first(x, z, value):
        first[x, z] = value

    def put_second(x, z, value):
        second[x, z] = value

    unroll = 10
    steps = -(-(wide + total - 4) // unroll)
    wrap_strips(shifted)
    advance(shifted, unroll, steps, put_first)
    wrap_strips(first)
    advance(first, unroll, steps, put_second)

    begins = lane < STRIP // 2

    def put_rows(step, carry):
        for k in range(8):
            row = GHOST + 8 * step + k
            group = jnp.int32(0)
            for j in range(1, groups - 1):
                group = group + (row + shifts.base > cap * j).astype(jnp.int32)
            i = row + shifts.base - cap * group
            turn = (span - STRIP * group - GHOST) & (span - 1)
            for z in range(planes):
                head = pltpu.roll(shifted[1 + i, z] + second[1 + i, z], turn, 1)
                body = pltpu.roll(shifted[wide + row, z] + second[wide + row, z], GHOST, 1)
                out[pl.ds(row - GHOST + z * nx, nfields, stride=planes * nx), :] = 0.5 * jnp.where(
                    begins, head, body
                )
        return carry

    lax.fori_loop(0, nx // 8, put_rows, 0)


def per_device(state, offsets, fraction, speeds, coupling):
    nfields, planes, nx, span = state.shape
    devices = lax.axis_size("az")
    cap = rows_per_block(devices)
    total = nx + 2 * GHOST
    few = total % cap
    groups = total // cap + 3
    vmem = pl.BlockSpec(memory_space=pltpu.VMEM)
    smem = pl.BlockSpec(memory_space=pltpu.SMEM)
    sizes = [cap] + [cap + 1] * (groups - 2) + [few]
    *sent, key = pl.pallas_call(
        functools.partial(pack_kernel, cap, nx, planes, devices),
        out_shape=[jax.ShapeDtypeStruct((n, planes, nfields, span), jnp.float32) for n in sizes]
        + [jax.ShapeDtypeStruct((1,), jnp.int32)],
        in_specs=[smem, vmem],
        out_specs=[vmem] * groups + [smem],
        name="pack",
    )(offsets, state.reshape(nfields * planes * nx, span))

    def branch(block, count):
        def send(*parts):
            received = []
            for j, part in enumerate(parts):
                steps = (block + j) % devices
                if steps and j < count:
                    part = lax.ppermute(
                        part, "az", [(i, (i + steps) % devices) for i in range(devices)]
                    )
                received.append(part)
            return received

        return send

    branches = [branch(block, count) for block in range(devices) for count in (groups - 1, groups)]
    arrived = lax.switch(key[0], branches, *sent)

    rows = cap + 5 + total + 13
    out = pl.pallas_call(
        functools.partial(step_kernel, cap, nx, planes, groups),
        out_shape=jax.ShapeDtypeStruct((nfields * planes * nx, span), jnp.float32),
        in_specs=[smem, smem, vmem, vmem] + [vmem] * groups,
        out_specs=vmem,
        scratch_shapes=[pltpu.VMEM((rows, planes, nfields, span), jnp.float32)] * 3,
        name="step",
    )(offsets, fraction, speeds, coupling, *arrived)
    return out.reshape(state.shape)


def solution(mesh):
    return jax.shard_map(
        per_device,
        mesh=mesh,
        in_specs=(P(None, "runs", None, "az"), P("runs"), P("runs"), P(), P()),
        out_specs=P(None, "runs", None, "az"),
        check_vma=False,
    )
```

```python
import functools

import jax
import jax.numpy as jnp
from jax import lax
from jax.experimental import pallas as pl
from jax.experimental.pallas import tpu as pltpu
from jax.sharding import PartitionSpec as P

courant = 0.3
GHOST = 4
EDGE = 2 * GHOST + 1
STRIP = 4 * GHOST


def rows_per_block(devices):
    return 9 if devices <= 16 else 6


class Shifts:
    def __init__(self, offs, cap, span):
        self.offs, self.cap, self.span = offs, cap, span
        start = self.within(0)
        late = [(self.within(m) < start).astype(jnp.int32) for m in range(1, cap)]
        self.base = functools.reduce(lambda a, b: a + b, late) + 1

    def within(self, x):
        return (self.offs[x] + (self.span - GHOST)) & (self.span - 1)

    def of_slot(self, i):
        return self.within(jnp.where(i < self.base, i + self.cap, i) - self.base)


def step_weights(speeds, coupling, tile):
    nfields = tile[0]
    rows = lax.broadcasted_iota(jnp.int32, (nfields, nfields), 0)
    cols = lax.broadcasted_iota(jnp.int32, (nfields, nfields), 1)

    def spread(picked):
        return jnp.broadcast_to(jnp.sum(picked, axis=1, keepdims=True), tile)

    terms = []
    for axis in range(3):
        speed = spread(jnp.where(rows == cols, speeds[axis : axis + 1, :], 0.0))
        slope_part = jnp.where(
            speed > 0.0, 0.5 * (1.0 - courant * speed), -0.5 * (1.0 + courant * speed)
        )
        scaled = -courant * speed
        terms += [scaled, scaled * slope_part, speed]
    for r in range(nfields):
        mixed = courant * spread(jnp.where((rows - cols) % nfields == r, coupling[...], 0.0))
        terms.append(mixed + 1.0 if r == 0 else mixed)
    return terms


def pack_kernel(cap, nx, planes, devices, *refs):
    operands, refs = refs[:4], refs[4:]
    held, refs, sem = refs[-5:-1], refs[:-5], refs[-1]
    copies = [pltpu.make_async_copy(a, b, sem.at[n]) for n, (a, b) in enumerate(zip(operands, held))]
    for copy in copies:
        copy.start()
    offs, speeds, coupling, cells = held
    groups = len(refs) - 2
    sent, (key, weights) = refs[:groups], refs[groups:]
    nfields, span = sent[0].shape[2:]
    tile = (nfields, span)
    copies[0].wait()
    shifts = Shifts(offs, cap, span)
    few = sent[-1].shape[0]
    block = ((offs[0] + (devices * span - GHOST)) >> (span.bit_length() - 1)) & (devices - 1)
    key[0] = 2 * block + (shifts.base >= cap + 1 - few).astype(jnp.int32)
    copies[1].wait()
    copies[2].wait()
    for t, term in enumerate(step_weights(speeds, coupling, tile)):
        weights[t] = term
    lane = lax.broadcasted_iota(jnp.int32, tile, 1)
    copies[3].wait()

    def row(i, k, z):
        x = cap * k + i - shifts.base
        source = jnp.where(x < GHOST, x + nx, x) - GHOST
        source = jnp.where(source >= nx, source - nx, source)
        return cells[pl.ds(jnp.clip(source, 0, nx - 1) + z * nx, nfields, stride=planes * nx), :]

    def one_slot(i, carry):
        edges, nearer = carry
        within = shifts.of_slot(i)
        near = lane >= within
        offset = lane - EDGE * (i - 1)
        member = (offset >= 0) & (offset < EDGE)
        nearer = jnp.where(member, (offset + (span - EDGE) >= within).astype(jnp.int32), nearer)
        new = []
        for z in range(planes):
            before = None
            for k in range(groups - 1):
                rows = row(i, k, z)
                value = pltpu.roll(rows, within, 1)
                sent[k][i - 1 if k == 0 else i, z] = value if k == 0 else jnp.where(near, value, before)
                piece = pltpu.roll(rows, (within + EDGE * i) & (span - 1), 1)
                new.append(jnp.where(member, piece, edges[z * (groups - 1) + k]))
                before = value
        return tuple(new), nearer

    zero = jnp.zeros(tile, jnp.float32)
    carry = (zero,) * (planes * (groups - 1)), jnp.zeros(tile, jnp.int32)
    for i in range(1, cap + 1):
        carry = one_slot(i, carry)
    edges, nearer = carry[0], carry[1] > 0
    for z in range(planes):
        for i in range(1, few):
            sent[-1][i, z] = pltpu.roll(row(i, groups - 2, z), shifts.of_slot(i), 1)
        for j in range(1, groups):
            near_edge = edges[z * (groups - 1) + j - 1]
            far_edge = edges[z * (groups - 1) + max(j - 2, 0)]
            sent[j][0, z] = jnp.where(nearer, near_edge, far_edge)


def minmod(lower, upper):
    return jnp.maximum(jnp.minimum(upper, 0.0), jnp.minimum(lower, jnp.maximum(upper, 0.0)))


def step_kernel(cap, nx, planes, groups, offs, frac, weights, *refs):
    arrived = refs[:groups]
    out, shifted, first, second, rows_out, sem = refs[groups:]
    nfields, span = arrived[0].shape[2:]
    total = nx + 2 * GHOST
    few = arrived[-1].shape[0]
    tile = (nfields, span)
    wide = cap + 5
    shifts = Shifts(offs, cap, span)
    lane = lax.broadcasted_iota(jnp.int32, tile, 1)
    slot = lane // STRIP
    lower_half = lane < span // 2
    first_lane = lane == 0

    terms = [weights[t] for t in range(9 + nfields)]
    sx, tx, ax, sy, ty, ay, sz, tz, az = terms[:9]
    px, py, pz = ax > 0.0, ay > 0.0, az > 0.0
    mix = terms[9:]

    def remap_slot(i):
        within = shifts.of_slot(i)
        near = lane >= within
        nearer = lane >= within + (EDGE * i - span)
        for z in range(planes):
            strip = None
            for k in range(groups - 1):
                x = jnp.clip(cap * k + i - shifts.base, -1, total)
                f = frac[jnp.clip(x, 0, total - 1)]
                here = arrived[k][i - 1 if k == 0 else i, z]
                after = arrived[k + 1][i if k + 2 < groups else jnp.minimum(i, few - 1), z]
                upper = jnp.where(near, here, after)
                ends = arrived[k + 1][0, z]
                if k + 2 < groups:
                    ends = jnp.where(nearer, ends, arrived[k + 2][0, z])
                edge = pltpu.roll(ends, span - EDGE * i, 1)
                edge_lower = pltpu.roll(ends, span - EDGE * i + 1, 1)
                lower = jnp.where(first_lane, edge_lower, pltpu.roll(upper, 1, 1))
                body = (1.0 - f) * upper + f * lower
                edge = (1.0 - f) * edge + f * edge_lower
                shifted[wide + x, z] = body
                piece = pltpu.roll(
                    jnp.where(lower_half, body, edge), (STRIP * k + STRIP // 2) % span, 1
                )
                strip = piece if k == 0 else jnp.where(slot == k, piece, strip)
            shifted[1 + i, z] = strip

    def remap_slots(step, carry):
        for u in range(3):
            remap_slot(3 * step + u + 1)
        return carry

    lax.fori_loop(0, cap // 3, remap_slots, 0)

    def wrap_strips(ref):
        for z in range(planes):
            for i in range(2):
                ref[i, z] = pltpu.roll(ref[i + cap, z], STRIP, 1)
                ref[2 + cap + i, z] = pltpu.roll(ref[2 + i, z], span - STRIP, 1)

    def state_of(u, before, after):
        return sx * u + tx * minmod(before, after)

    def advance(source, unroll, steps, emit):
        def enter(z):
            u = [source[i, z] for i in range(4)]
            jumps = [u[i + 1] - u[i] for i in range(3)]
            low = state_of(u[1], jumps[0], jumps[1])
            here = state_of(u[2], jumps[1], jumps[2])
            return u[2], u[3], jumps[2], here, here - low

        def body(step, carry):
            for k in range(unroll):
                x = 2 + step * unroll + k
                vertical = []
                for z in range(planes):
                    u = carry[z][0]
                    above, below = carry[(z + 1) % planes][0], carry[(z - 1) % planes][0]
                    vertical.append(sz * u + tz * minmod(u - below, above - u))
                following = []
                for z in range(planes):
                    u, ahead_u, jump, here, behind_face = carry[z]
                    beyond = source[x + 2, z]
                    next_jump = beyond - ahead_u
                    there = state_of(ahead_u, jump, next_jump)
                    face = there - here
                    following.append((ahead_u, beyond, next_jump, there, face))
                    value = mix[0] * u + jnp.where(px, behind_face, face)
                    for r in range(1, nfields):
                        value = value + mix[r] * pltpu.roll(u, r, 0)
                    value = value + jnp.where(
                        pz,
                        vertical[z] - vertical[(z - 1) % planes],
                        vertical[(z + 1) % planes] - vertical[z],
                    )
                    near = [pltpu.roll(u, shift % span, 1) if shift else u for shift in (2, 1, 0, -1, -2)]
                    near = [jnp.where(py, near[j], near[j + 1]) for j in range(4)]
                    steps_y = [near[j + 1] - near[j] for j in range(3)]
                    side = sy * steps_y[1] + ty * (
                        minmod(steps_y[1], steps_y[2]) - minmod(steps_y[0], steps_y[1])
                    )
                    emit(x, z, value + side)
                carry = tuple(following)
            return carry

        lax.fori_loop(0, steps, body, tuple(enter(z) for z in range(planes)))

    def put_first(x, z, value):
        first[x, z] = value

    def put_second(x, z, value):
        second[x, z] = value

    unroll = 10
    steps = -(-(wide + total - 4) // unroll)
    wrap_strips(shifted)
    advance(shifted, unroll, steps, put_first)
    wrap_strips(first)
    advance(first, unroll, steps, put_second)

    begins = lane < STRIP // 2

    by_row = rows_out.reshape(nfields * planes, nx, span)
    some = 8

    def piece_of(step):
        part = pl.ds(pl.multiple_of(some * step, some), some)
        return pltpu.make_async_copy(by_row.at[:, part], out.at[:, part], sem.at[step])

    def put_rows(step, carry):
        for k in range(some):
            row = GHOST + some * step + k
            group = jnp.int32(0)
            for j in range(1, groups - 1):
                group = group + (row + shifts.base > cap * j).astype(jnp.int32)
            i = row + shifts.base - cap * group
            turn = (span - STRIP * group - GHOST) & (span - 1)
            for z in range(planes):
                head = pltpu.roll(shifted[1 + i, z] + second[1 + i, z], turn, 1)
                body = pltpu.roll(shifted[wide + row, z] + second[wide + row, z], GHOST, 1)
                at = pl.ds(row - GHOST + z * nx, nfields, stride=planes * nx)
                rows_out[at, :] = 0.5 * jnp.where(begins, head, body)
        piece_of(step).start()
        return carry

    lax.fori_loop(0, nx // some, put_rows, 0)
    for step in range(nx // some):
        piece_of(step).wait()


def per_device(state, offsets, fraction, speeds, coupling):
    nfields, planes, nx, span = state.shape
    devices = lax.axis_size("az")
    cap = rows_per_block(devices)
    total = nx + 2 * GHOST
    few = total % cap
    groups = total // cap + 3
    vmem = pl.BlockSpec(memory_space=pltpu.VMEM)
    smem = pl.BlockSpec(memory_space=pltpu.SMEM)
    hbm = pl.BlockSpec(memory_space=pl.ANY)
    sizes = [cap] + [cap + 1] * (groups - 2) + [few]
    *sent, key, weights = pl.pallas_call(
        functools.partial(pack_kernel, cap, nx, planes, devices),
        out_shape=[jax.ShapeDtypeStruct((n, planes, nfields, span), jnp.float32) for n in sizes]
        + [
            jax.ShapeDtypeStruct((1,), jnp.int32),
            jax.ShapeDtypeStruct((9 + nfields, nfields, span), jnp.float32),
        ],
        in_specs=[hbm] * 4,
        out_specs=[vmem] * groups + [smem, vmem],
        scratch_shapes=[
            pltpu.SMEM(offsets.shape, jnp.int32),
            pltpu.VMEM(speeds.shape, jnp.float32),
            pltpu.VMEM(coupling.shape, jnp.float32),
            pltpu.VMEM((nfields * planes * nx, span), jnp.float32),
            pltpu.SemaphoreType.DMA((4,)),
        ],
        name="pack",
    )(offsets, speeds, coupling, state.reshape(nfields * planes * nx, span))

    order = sorted(range(groups), key=lambda j: (j in (0, groups - 1), abs(2 * j - groups + 1)))

    def branch(block, count):
        def send(*parts):
            received = []
            for j in order:
                steps = (block + j) % devices
                part = parts[j]
                if steps and j < count:
                    part = lax.ppermute(
                        part, "az", [(i, (i + steps) % devices) for i in range(devices)]
                    )
                received.append(part)
            return received

        return send

    branches = [branch(block, count) for block in range(devices) for count in (groups - 1, groups)]
    arrived = lax.switch(key[0], branches, *sent)
    arrived = [arrived[order.index(j)] for j in range(groups)]

    rows = cap + 5 + total + 13
    out = pl.pallas_call(
        functools.partial(step_kernel, cap, nx, planes, groups),
        out_shape=jax.ShapeDtypeStruct((nfields * planes, nx, span), jnp.float32),
        in_specs=[smem, smem, vmem] + [vmem] * groups,
        out_specs=hbm,
        scratch_shapes=[pltpu.VMEM((rows, planes, nfields, span), jnp.float32)] * 3
        + [
            pltpu.VMEM((nfields * planes * nx, span), jnp.float32),
            pltpu.SemaphoreType.DMA((nx // 8,)),
        ],
        name="step",
    )(offsets, fraction, weights, *arrived)
    return out.reshape(state.shape)


def solution(mesh):
    return jax.shard_map(
        per_device,
        mesh=mesh,
        in_specs=(P(None, "runs", None, "az"), P("runs"), P("runs"), P(), P()),
        out_specs=P(None, "runs", None, "az"),
        check_vma=False,
    )
```

```python
import functools

import jax
import jax.numpy as jnp
from jax import lax
from jax.experimental import pallas as pl
from jax.experimental.pallas import tpu as pltpu
from jax.sharding import PartitionSpec as P

courant = 0.3
GHOST = 4
EDGE = 2 * GHOST + 1
STRIP = 4 * GHOST


def rows_per_block(devices):
    return 9 if devices <= 16 else 6


class Shifts:
    def __init__(self, offs, cap, span):
        self.offs, self.cap, self.span = offs, cap, span
        start = self.within(0)
        late = [(self.within(m) < start).astype(jnp.int32) for m in range(1, cap)]
        self.base = functools.reduce(lambda a, b: a + b, late) + 1

    def within(self, x):
        return (self.offs[x] + (self.span - GHOST)) & (self.span - 1)

    def of_slot(self, i):
        return self.within(jnp.where(i < self.base, i + self.cap, i) - self.base)


def paired(low, high, together):
    rows, left = [], list(range(high, low - 1, -1))
    while left:
        i = left.pop(0)
        other = together - i
        if other in left:
            left.remove(other)
            rows.append((i, other))
        else:
            rows.append((i, None))
    return rows


class Messages:
    def __init__(self, cap, total):
        few = total % cap
        self.last = total // cap + 1
        self.begin = paired(1, cap, cap + 3)
        self.end = paired(1, cap - 1, cap)
        self.first = paired(cap - few + 1, cap, 2 * cap - few + 1)
        self.over = paired(1, few - 1, few)
        self.few = few
        self.sizes = [cap + 1] * self.last + [
            len(self.begin),
            1 + len(self.end),
            len(self.first) + 1 + len(self.over),
        ]
        full = [[(cap + 1, j)] for j in range(1, self.last)]
        pieces = [(len(self.first), 0), (1 + len(self.over), self.last + 1)]
        self.moves = [
            full + [[], [(len(self.begin), 0)], [(1 + len(self.end), self.last)], []],
            full + [[(cap + 1, self.last)], [], [], pieces],
        ]


def step_weights(speeds, coupling, tile):
    nfields = tile[0]
    rows = lax.broadcasted_iota(jnp.int32, (nfields, nfields), 0)
    cols = lax.broadcasted_iota(jnp.int32, (nfields, nfields), 1)

    def spread(picked):
        return jnp.broadcast_to(jnp.sum(picked, axis=1, keepdims=True), tile)

    terms = []
    for axis in range(3):
        speed = spread(jnp.where(rows == cols, speeds[axis : axis + 1, :], 0.0))
        slope_part = jnp.where(
            speed > 0.0, 0.5 * (1.0 - courant * speed), -0.5 * (1.0 + courant * speed)
        )
        scaled = -courant * speed
        terms += [scaled, scaled * slope_part, speed]
    for r in range(nfields):
        mixed = courant * spread(jnp.where((rows - cols) % nfields == r, coupling[...], 0.0))
        terms.append(mixed + 1.0 if r == 0 else mixed)
    return terms


def pack_kernel(cap, nx, planes, devices, *refs):
    operands, refs = refs[:4], refs[4:]
    held, refs, sem = refs[-5:-1], refs[:-5], refs[-1]
    copies = [pltpu.make_async_copy(a, b, sem.at[n]) for n, (a, b) in enumerate(zip(operands, held))]
    for copy in copies:
        copy.start()
    offs, speeds, coupling, cells = held
    sent, (key, weights) = refs[:-2], refs[-2:]
    nfields, span = sent[0].shape[2:]
    plan = Messages(cap, nx + 2 * GHOST)
    full, (begin, end, rest) = sent[:-3], sent[-3:]
    last, split = plan.last, len(plan.first)
    tile = (nfields, span)
    copies[0].wait()
    shifts = Shifts(offs, cap, span)
    block = ((offs[0] + (devices * span - GHOST)) >> (span.bit_length() - 1)) & (devices - 1)
    key[0] = 2 * block + (shifts.base >= cap + 1 - plan.few).astype(jnp.int32)
    copies[1].wait()
    copies[2].wait()
    for t, term in enumerate(step_weights(speeds, coupling, tile)):
        weights[t] = term
    lane = lax.broadcasted_iota(jnp.int32, tile, 1)
    copies[3].wait()

    def row(i, k, z):
        x = cap * k + i - shifts.base
        source = jnp.where(x < GHOST, x + nx, x) - GHOST
        source = jnp.where(source >= nx, source - nx, source)
        return cells[pl.ds(jnp.clip(source, 0, nx - 1) + z * nx, nfields, stride=planes * nx), :]

    def one_slot(i, carry):
        edges, nearer = carry
        within = shifts.of_slot(i)
        near = lane >= within
        offset = lane - EDGE * (i - 1)
        member = (offset >= 0) & (offset < EDGE)
        nearer = jnp.where(member, (offset + (span - EDGE) >= within).astype(jnp.int32), nearer)
        new = []
        for z in range(planes):
            before = None
            for k in range(last + 1):
                rows = row(i, k, z)
                value = pltpu.roll(rows, within, 1)
                if k:
                    full[k - 1][i, z] = jnp.where(near, value, before)
                piece = pltpu.roll(rows, (within + EDGE * i) & (span - 1), 1)
                new.append(jnp.where(member, piece, edges[z * (last + 1) + k]))
                before = value
        return tuple(new), nearer

    zero = jnp.zeros(tile, jnp.float32)
    carry = (zero,) * (planes * (last + 1)), jnp.zeros(tile, jnp.int32)
    for i in range(1, cap + 1):
        carry = one_slot(i, carry)
    edges, nearer = carry[0], carry[1] > 0
    for z in range(planes):
        for ref, pairs, k, at, below in (
            (begin, plan.begin, 0, 0, False),
            (end, plan.end, last - 1, 1, True),
            (rest, plan.first, 0, 0, False),
            (rest, plan.over, last, split + 1, True),
        ):
            for n, (i, other) in enumerate(pairs):
                within = shifts.of_slot(i)
                value = pltpu.roll(row(i, k, z), within, 1)
                if other is not None:
                    used = lane < within if below else lane >= within
                    value = jnp.where(used, value, row(other, k, z))
                ref[at + n, z] = value
        for j in range(1, last + 2):
            near_edge = edges[z * (last + 1) + j - 1]
            far_edge = edges[z * (last + 1) + max(j - 2, 0)]
            ends = jnp.where(nearer, near_edge, far_edge)
            if j <= last:
                full[j - 1][0, z] = ends
            if j == last:
                end[0, z] = ends
            if j > last:
                rest[split, z] = ends


def minmod(lower, upper):
    return jnp.maximum(jnp.minimum(upper, 0.0), jnp.minimum(lower, jnp.maximum(upper, 0.0)))


def step_kernel(cap, nx, planes, offs, frac, weights, *refs):
    arrived, (out, shifted, first, second, rows_out, sem) = refs[:-6], refs[-6:]
    nfields, span = arrived[0].shape[2:]
    total = nx + 2 * GHOST
    plan = Messages(cap, total)
    last = plan.last
    full, (begin, end, rest) = arrived[:-3], arrived[-3:]
    split = len(plan.first)
    tile = (nfields, span)
    wide = cap + 5
    shifts = Shifts(offs, cap, span)
    lane = lax.broadcasted_iota(jnp.int32, tile, 1)
    slot = lane // STRIP
    lower_half = lane < span // 2
    first_lane = lane == 0

    terms = [weights[t] for t in range(9 + nfields)]
    sx, tx, ax, sy, ty, ay, sz, tz, az = terms[:9]
    px, py, pz = ax > 0.0, ay > 0.0, az > 0.0
    mix = terms[9:]

    many = shifts.base >= cap + 1 - plan.few

    def place(i, pairs, at):
        row, raw = jnp.int32(0), jnp.int32(0)
        for n, (a, b) in enumerate(pairs):
            row = jnp.where(i == a, at + n, row)
            if b is not None:
                row = jnp.where(i == b, at + n, row)
                raw = jnp.where(i == b, 1, raw)
        return row, raw

    def remap_slot(i):
        within = shifts.of_slot(i)
        near = lane >= within
        nearer = lane >= within + (EDGE * i - span)
        begin_row, begin_raw = place(i, plan.begin, 0)
        many_row, many_raw = place(i, plan.first, 0)
        end_row, end_raw = place(i, plan.end, 1)
        over_row, over_raw = place(i, plan.over, split + 1)
        begin_turn = jnp.where(many, many_raw, begin_raw) * within
        end_turn = jnp.where(many, 0, end_raw) * within
        for z in range(planes):
            strip = None
            mains = [
                pltpu.roll(
                    jnp.where(many, rest[many_row, z], begin[begin_row, z]), begin_turn, 1
                )
            ]
            tails = [None]
            for k in range(1, last):
                mains.append(full[k - 1][i, z])
                tails.append(full[k - 1][0, z])
            mains.append(
                pltpu.roll(jnp.where(many, full[last - 1][i, z], end[end_row, z]), end_turn, 1)
            )
            tails.append(jnp.where(many, full[last - 1][0, z], end[0, z]))
            mains.append(pltpu.roll(rest[over_row, z], over_raw * within, 1))
            tails.append(rest[split, z])
            for k in range(last + 1):
                x = jnp.clip(cap * k + i - shifts.base, -1, total)
                f = frac[jnp.clip(x, 0, total - 1)]
                upper = jnp.where(near, mains[k], mains[k + 1])
                ends = tails[k + 1]
                if k < last:
                    ends = jnp.where(nearer, ends, tails[k + 2])
                edge = pltpu.roll(ends, span - EDGE * i, 1)
                edge_lower = pltpu.roll(ends, span - EDGE * i + 1, 1)
                lower = jnp.where(first_lane, edge_lower, pltpu.roll(upper, 1, 1))
                body = (1.0 - f) * upper + f * lower
                edge = (1.0 - f) * edge + f * edge_lower
                shifted[wide + x, z] = body
                piece = pltpu.roll(
                    jnp.where(lower_half, body, edge), (STRIP * k + STRIP // 2) % span, 1
                )
                strip = piece if k == 0 else jnp.where(slot == k, piece, strip)
            shifted[1 + i, z] = strip

    def remap_slots(step, carry):
        for u in range(3):
            remap_slot(3 * step + u + 1)
        return carry

    lax.fori_loop(0, cap // 3, remap_slots, 0)

    def wrap_strips(ref):
        for z in range(planes):
            for i in range(2):
                ref[i, z] = pltpu.roll(ref[i + cap, z], STRIP, 1)
                ref[2 + cap + i, z] = pltpu.roll(ref[2 + i, z], span - STRIP, 1)

    def state_of(u, before, after):
        return sx * u + tx * minmod(before, after)

    def advance(source, unroll, steps, emit):
        def enter(z):
            u = [source[i, z] for i in range(4)]
            jumps = [u[i + 1] - u[i] for i in range(3)]
            low = state_of(u[1], jumps[0], jumps[1])
            here = state_of(u[2], jumps[1], jumps[2])
            return u[2], u[3], jumps[2], here, here - low

        def body(step, carry):
            for k in range(unroll):
                x = 2 + step * unroll + k
                vertical = []
                for z in range(planes):
                    u = carry[z][0]
                    above, below = carry[(z + 1) % planes][0], carry[(z - 1) % planes][0]
                    vertical.append(sz * u + tz * minmod(u - below, above - u))
                following = []
                for z in range(planes):
                    u, ahead_u, jump, here, behind_face = carry[z]
                    beyond = source[x + 2, z]
                    next_jump = beyond - ahead_u
                    there = state_of(ahead_u, jump, next_jump)
                    face = there - here
                    following.append((ahead_u, beyond, next_jump, there, face))
                    value = mix[0] * u + jnp.where(px, behind_face, face)
                    for r in range(1, nfields):
                        value = value + mix[r] * pltpu.roll(u, r, 0)
                    value = value + jnp.where(
                        pz,
                        vertical[z] - vertical[(z - 1) % planes],
                        vertical[(z + 1) % planes] - vertical[z],
                    )
                    near = [pltpu.roll(u, shift % span, 1) if shift else u for shift in (2, 1, 0, -1, -2)]
                    near = [jnp.where(py, near[j], near[j + 1]) for j in range(4)]
                    steps_y = [near[j + 1] - near[j] for j in range(3)]
                    side = sy * steps_y[1] + ty * (
                        minmod(steps_y[1], steps_y[2]) - minmod(steps_y[0], steps_y[1])
                    )
                    emit(x, z, value + side)
                carry = tuple(following)
            return carry

        lax.fori_loop(0, steps, body, tuple(enter(z) for z in range(planes)))

    def put_first(x, z, value):
        first[x, z] = value

    def put_second(x, z, value):
        second[x, z] = value

    unroll = 10
    steps = -(-(wide + total - 4) // unroll)
    wrap_strips(shifted)
    advance(shifted, unroll, steps, put_first)
    wrap_strips(first)
    advance(first, unroll, steps, put_second)

    begins = lane < STRIP // 2

    by_row = rows_out.reshape(nfields * planes, nx, span)
    some = 8

    def piece_of(step):
        part = pl.ds(pl.multiple_of(some * step, some), some)
        return pltpu.make_async_copy(by_row.at[:, part], out.at[:, part], sem.at[step])

    def put_rows(step, carry):
        for k in range(some):
            row = GHOST + some * step + k
            group = jnp.int32(0)
            for j in range(1, last + 1):
                group = group + (row + shifts.base > cap * j).astype(jnp.int32)
            i = row + shifts.base - cap * group
            turn = (span - STRIP * group - GHOST) & (span - 1)
            for z in range(planes):
                head = pltpu.roll(shifted[1 + i, z] + second[1 + i, z], turn, 1)
                body = pltpu.roll(shifted[wide + row, z] + second[wide + row, z], GHOST, 1)
                at = pl.ds(row - GHOST + z * nx, nfields, stride=planes * nx)
                rows_out[at, :] = 0.5 * jnp.where(begins, head, body)
        piece_of(step).start()
        return carry

    lax.fori_loop(0, nx // some, put_rows, 0)
    for step in range(nx // some):
        piece_of(step).wait()


def per_device(state, offsets, fraction, speeds, coupling):
    nfields, planes, nx, span = state.shape
    devices = lax.axis_size("az")
    cap = rows_per_block(devices)
    total = nx + 2 * GHOST
    plan = Messages(cap, total)
    count = len(plan.sizes)
    vmem = pl.BlockSpec(memory_space=pltpu.VMEM)
    smem = pl.BlockSpec(memory_space=pltpu.SMEM)
    hbm = pl.BlockSpec(memory_space=pl.ANY)
    *sent, key, weights = pl.pallas_call(
        functools.partial(pack_kernel, cap, nx, planes, devices),
        out_shape=[jax.ShapeDtypeStruct((n, planes, nfields, span), jnp.float32) for n in plan.sizes]
        + [
            jax.ShapeDtypeStruct((1,), jnp.int32),
            jax.ShapeDtypeStruct((9 + nfields, nfields, span), jnp.float32),
        ],
        in_specs=[hbm] * 4,
        out_specs=[vmem] * count + [smem, vmem],
        scratch_shapes=[
            pltpu.SMEM(offsets.shape, jnp.int32),
            pltpu.VMEM(speeds.shape, jnp.float32),
            pltpu.VMEM(coupling.shape, jnp.float32),
            pltpu.VMEM((nfields * planes * nx, span), jnp.float32),
            pltpu.SemaphoreType.DMA((4,)),
        ],
        name="pack",
    )(offsets, speeds, coupling, state.reshape(nfields * planes * nx, span))

    order = [plan.last] + list(range(plan.last)) + [plan.last + 1, plan.last + 2]

    def branch(block, moves):
        def send(*parts):
            received = []
            for n in order:
                part, at = parts[n], 0
                pieces = []
                for size, group in moves[n]:
                    steps = (block + group) % devices
                    piece = part[at : at + size]
                    if steps:
                        piece = lax.ppermute(
                            piece, "az", [(i, (i + steps) % devices) for i in range(devices)]
                        )
                    pieces.append(piece)
                    at += size
                received.append(jnp.concatenate(pieces, axis=0) if pieces else part)
            return received

        return send

    branches = [branch(block, moves) for block in range(devices) for moves in plan.moves]
    arrived = lax.switch(key[0], branches, *sent)
    arrived = [arrived[order.index(n)] for n in range(count)]

    rows = cap + 5 + total + 13
    out = pl.pallas_call(
        functools.partial(step_kernel, cap, nx, planes),
        out_shape=jax.ShapeDtypeStruct((nfields * planes, nx, span), jnp.float32),
        in_specs=[smem, smem, vmem] + [vmem] * count,
        out_specs=hbm,
        scratch_shapes=[pltpu.VMEM((rows, planes, nfields, span), jnp.float32)] * 3
        + [
            pltpu.VMEM((nfields * planes * nx, span), jnp.float32),
            pltpu.SemaphoreType.DMA((nx // 8,)),
        ],
        name="step",
    )(offsets, fraction, weights, *arrived)
    return out.reshape(state.shape)


def solution(mesh):
    return jax.shard_map(
        per_device,
        mesh=mesh,
        in_specs=(P(None, "runs", None, "az"), P("runs"), P("runs"), P(), P()),
        out_specs=P(None, "runs", None, "az"),
        check_vma=False,
    )
```

```python
import functools

import jax
import jax.numpy as jnp
from jax import lax
from jax.experimental import pallas as pl
from jax.experimental.pallas import tpu as pltpu
from jax.sharding import PartitionSpec as P

courant = 0.3
GHOST = 4
EDGE = 2 * GHOST + 1
OUT_ROWS = 16
STRIP = 4 * GHOST


def rows_per_block(devices):
    return 9 if devices <= 16 else 6


class Shifts:
    def __init__(self, offs, cap, span):
        self.offs, self.cap, self.span = offs, cap, span
        start = self.within(0)
        late = [(self.within(m) < start).astype(jnp.int32) for m in range(1, cap)]
        self.base = functools.reduce(lambda a, b: a + b, late) + 1

    def within(self, x):
        return (self.offs[x] + (self.span - GHOST)) & (self.span - 1)

    def of_slot(self, i):
        return self.within(jnp.where(i < self.base, i + self.cap, i) - self.base)


def paired(low, high, together):
    rows, left = [], list(range(high, low - 1, -1))
    while left:
        i = left.pop(0)
        other = together - i
        if other in left:
            left.remove(other)
            rows.append((i, other))
        else:
            rows.append((i, None))
    return rows


class Messages:
    def __init__(self, cap, total):
        few = total % cap
        self.last = total // cap + 1
        self.begin = paired(1, cap, cap + 3)
        self.end = paired(1, cap - 1, cap)
        self.first = paired(cap - few + 1, cap, 2 * cap - few + 1)
        self.over = paired(1, few - 1, few)
        self.few = few
        self.sizes = [cap + 1] * self.last + [
            len(self.begin),
            1 + len(self.end),
            len(self.first) + 1 + len(self.over),
        ]
        full = [[(cap + 1, j)] for j in range(1, self.last)]
        pieces = [(len(self.first), 0), (1 + len(self.over), self.last + 1)]
        self.moves = [
            full + [[], [(len(self.begin), 0)], [(1 + len(self.end), self.last)], []],
            full + [[(cap + 1, self.last)], [], [], pieces],
        ]


def step_weights(speeds, coupling, tile):
    nfields = tile[0]
    rows = lax.broadcasted_iota(jnp.int32, (nfields, nfields), 0)
    cols = lax.broadcasted_iota(jnp.int32, (nfields, nfields), 1)

    def spread(picked):
        return jnp.broadcast_to(jnp.sum(picked, axis=1, keepdims=True), tile)

    terms = []
    for axis in range(3):
        speed = spread(jnp.where(rows == cols, speeds[axis : axis + 1, :], 0.0))
        slope_part = jnp.where(
            speed > 0.0, 0.5 * (1.0 - courant * speed), -0.5 * (1.0 + courant * speed)
        )
        scaled = -courant * speed
        terms += [scaled, scaled * slope_part, speed]
    for r in range(nfields):
        mixed = courant * spread(jnp.where((rows - cols) % nfields == r, coupling[...], 0.0))
        terms.append(mixed + 1.0 if r == 0 else mixed)
    return terms


def pack_kernel(cap, nx, planes, devices, *refs):
    operands, refs = refs[:4], refs[4:]
    held, refs, sem = refs[-5:-1], refs[:-5], refs[-1]
    copies = [pltpu.make_async_copy(a, b, sem.at[n]) for n, (a, b) in enumerate(zip(operands, held))]
    for copy in copies:
        copy.start()
    offs, speeds, coupling, cells = held
    sent, (key, weights) = refs[:-2], refs[-2:]
    nfields, span = sent[0].shape[2:]
    plan = Messages(cap, nx + 2 * GHOST)
    full, (begin, end, rest) = sent[:-3], sent[-3:]
    last, split = plan.last, len(plan.first)
    tile = (nfields, span)
    copies[0].wait()
    shifts = Shifts(offs, cap, span)
    block = ((offs[0] + (devices * span - GHOST)) >> (span.bit_length() - 1)) & (devices - 1)
    key[0] = 2 * block + (shifts.base >= cap + 1 - plan.few).astype(jnp.int32)
    copies[1].wait()
    copies[2].wait()
    for t, term in enumerate(step_weights(speeds, coupling, tile)):
        weights[t] = term
    lane = lax.broadcasted_iota(jnp.int32, tile, 1)
    copies[3].wait()

    def row(i, k, z):
        x = cap * k + i - shifts.base
        source = jnp.where(x < GHOST, x + nx, x) - GHOST
        source = jnp.where(source >= nx, source - nx, source)
        return cells[pl.ds(jnp.clip(source, 0, nx - 1) + z * nx, nfields, stride=planes * nx), :]

    def one_slot(i, carry):
        edges, nearer = carry
        within = shifts.of_slot(i)
        near = lane >= within
        offset = lane - EDGE * (i - 1)
        member = (offset >= 0) & (offset < EDGE)
        nearer = jnp.where(member, (offset + (span - EDGE) >= within).astype(jnp.int32), nearer)
        new = []
        for z in range(planes):
            before = None
            for k in range(last + 1):
                rows = row(i, k, z)
                value = pltpu.roll(rows, within, 1)
                if k:
                    full[k - 1][i, z] = jnp.where(near, value, before)
                piece = pltpu.roll(rows, (within + EDGE * i) & (span - 1), 1)
                new.append(jnp.where(member, piece, edges[z * (last + 1) + k]))
                before = value
        return tuple(new), nearer

    zero = jnp.zeros(tile, jnp.float32)
    carry = (zero,) * (planes * (last + 1)), jnp.zeros(tile, jnp.int32)
    for i in range(1, cap + 1):
        carry = one_slot(i, carry)
    edges, nearer = carry[0], carry[1] > 0
    for z in range(planes):
        for ref, pairs, k, at, below in (
            (begin, plan.begin, 0, 0, False),
            (end, plan.end, last - 1, 1, True),
            (rest, plan.first, 0, 0, False),
            (rest, plan.over, last, split + 1, True),
        ):
            for n, (i, other) in enumerate(pairs):
                within = shifts.of_slot(i)
                value = pltpu.roll(row(i, k, z), within, 1)
                if other is not None:
                    used = lane < within if below else lane >= within
                    value = jnp.where(used, value, row(other, k, z))
                ref[at + n, z] = value
        for j in range(1, last + 2):
            near_edge = edges[z * (last + 1) + j - 1]
            far_edge = edges[z * (last + 1) + max(j - 2, 0)]
            ends = jnp.where(nearer, near_edge, far_edge)
            if j <= last:
                full[j - 1][0, z] = ends
            if j == last:
                end[0, z] = ends
            if j > last:
                rest[split, z] = ends


def minmod(lower, upper):
    return jnp.maximum(jnp.minimum(upper, 0.0), jnp.minimum(lower, jnp.maximum(upper, 0.0)))


def step_kernel(cap, nx, planes, offs, frac, weights, *refs):
    arrived, (out, shifted, first, second, rows_out, sem) = refs[:-6], refs[-6:]
    nfields, span = arrived[0].shape[2:]
    total = nx + 2 * GHOST
    plan = Messages(cap, total)
    last = plan.last
    full, (begin, end, rest) = arrived[:-3], arrived[-3:]
    split = len(plan.first)
    tile = (nfields, span)
    wide = cap + 5
    shifts = Shifts(offs, cap, span)
    lane = lax.broadcasted_iota(jnp.int32, tile, 1)
    slot = lane // STRIP
    lower_half = lane < span // 2
    first_lane = lane == 0

    terms = [weights[t] for t in range(9 + nfields)]
    sx, tx, ax, sy, ty, ay, sz, tz, az = terms[:9]
    px, py, pz = ax > 0.0, ay > 0.0, az > 0.0
    mix = terms[9:]

    many = shifts.base >= cap + 1 - plan.few

    def place(i, pairs, at):
        row, raw = jnp.int32(0), jnp.int32(0)
        for n, (a, b) in enumerate(pairs):
            row = jnp.where(i == a, at + n, row)
            if b is not None:
                row = jnp.where(i == b, at + n, row)
                raw = jnp.where(i == b, 1, raw)
        return row, raw

    def remap_slot(i):
        within = shifts.of_slot(i)
        near = lane >= within
        nearer = lane >= within + (EDGE * i - span)
        begin_row, begin_raw = place(i, plan.begin, 0)
        many_row, many_raw = place(i, plan.first, 0)
        end_row, end_raw = place(i, plan.end, 1)
        over_row, over_raw = place(i, plan.over, split + 1)
        begin_turn = jnp.where(many, many_raw, begin_raw) * within
        end_turn = jnp.where(many, 0, end_raw) * within
        for z in range(planes):
            strip = None
            mains = [
                pltpu.roll(
                    jnp.where(many, rest[many_row, z], begin[begin_row, z]), begin_turn, 1
                )
            ]
            tails = [None]
            for k in range(1, last):
                mains.append(full[k - 1][i, z])
                tails.append(full[k - 1][0, z])
            mains.append(
                pltpu.roll(jnp.where(many, full[last - 1][i, z], end[end_row, z]), end_turn, 1)
            )
            tails.append(jnp.where(many, full[last - 1][0, z], end[0, z]))
            mains.append(pltpu.roll(rest[over_row, z], over_raw * within, 1))
            tails.append(rest[split, z])
            for k in range(last + 1):
                x = jnp.clip(cap * k + i - shifts.base, -1, total)
                f = frac[jnp.clip(x, 0, total - 1)]
                upper = jnp.where(near, mains[k], mains[k + 1])
                ends = tails[k + 1]
                if k < last:
                    ends = jnp.where(nearer, ends, tails[k + 2])
                edge = pltpu.roll(ends, span - EDGE * i, 1)
                edge_lower = pltpu.roll(ends, span - EDGE * i + 1, 1)
                lower = jnp.where(first_lane, edge_lower, pltpu.roll(upper, 1, 1))
                body = (1.0 - f) * upper + f * lower
                edge = (1.0 - f) * edge + f * edge_lower
                shifted[wide + x, z] = body
                piece = pltpu.roll(
                    jnp.where(lower_half, body, edge), (STRIP * k + STRIP // 2) % span, 1
                )
                strip = piece if k == 0 else jnp.where(slot == k, piece, strip)
            shifted[1 + i, z] = strip

    def remap_slots(step, carry):
        for u in range(3):
            remap_slot(3 * step + u + 1)
        return carry

    lax.fori_loop(0, cap // 3, remap_slots, 0)

    def wrap_strips(ref):
        for z in range(planes):
            for i in range(2):
                ref[i, z] = pltpu.roll(ref[i + cap, z], STRIP, 1)
                ref[2 + cap + i, z] = pltpu.roll(ref[2 + i, z], span - STRIP, 1)

    def state_of(u, before, after):
        return sx * u + tx * minmod(before, after)

    def advance(source, unroll, steps, emit):
        def enter(z):
            u = [source[i, z] for i in range(4)]
            jumps = [u[i + 1] - u[i] for i in range(3)]
            low = state_of(u[1], jumps[0], jumps[1])
            here = state_of(u[2], jumps[1], jumps[2])
            return u[2], u[3], jumps[2], here, here - low

        def body(step, carry):
            for k in range(unroll):
                x = 2 + step * unroll + k
                vertical = []
                for z in range(planes):
                    u = carry[z][0]
                    above, below = carry[(z + 1) % planes][0], carry[(z - 1) % planes][0]
                    vertical.append(sz * u + tz * minmod(u - below, above - u))
                following = []
                for z in range(planes):
                    u, ahead_u, jump, here, behind_face = carry[z]
                    beyond = source[x + 2, z]
                    next_jump = beyond - ahead_u
                    there = state_of(ahead_u, jump, next_jump)
                    face = there - here
                    following.append((ahead_u, beyond, next_jump, there, face))
                    value = mix[0] * u + jnp.where(px, behind_face, face)
                    for r in range(1, nfields):
                        value = value + mix[r] * pltpu.roll(u, r, 0)
                    value = value + jnp.where(
                        pz,
                        vertical[z] - vertical[(z - 1) % planes],
                        vertical[(z + 1) % planes] - vertical[z],
                    )
                    near = [pltpu.roll(u, shift % span, 1) if shift else u for shift in (2, 1, 0, -1, -2)]
                    near = [jnp.where(py, near[j], near[j + 1]) for j in range(4)]
                    steps_y = [near[j + 1] - near[j] for j in range(3)]
                    side = sy * steps_y[1] + ty * (
                        minmod(steps_y[1], steps_y[2]) - minmod(steps_y[0], steps_y[1])
                    )
                    emit(x, z, value + side)
                carry = tuple(following)
            return carry

        lax.fori_loop(0, steps, body, tuple(enter(z) for z in range(planes)))

    def put_first(x, z, value):
        first[x, z] = value

    def put_second(x, z, value):
        second[x, z] = value

    unroll = 10
    steps = -(-(wide + total - 4) // unroll)
    wrap_strips(shifted)
    advance(shifted, unroll, steps, put_first)
    wrap_strips(first)
    advance(first, unroll, steps, put_second)

    begins = lane < STRIP // 2

    by_row = rows_out.reshape(nfields * planes, nx, span)
    some = OUT_ROWS

    def piece_of(step):
        part = pl.ds(pl.multiple_of(some * step, some), some)
        return pltpu.make_async_copy(by_row.at[:, part], out.at[:, part], sem.at[step])

    def put_rows(step, carry):
        for k in range(some):
            row = GHOST + some * step + k
            group = jnp.int32(0)
            for j in range(1, last + 1):
                group = group + (row + shifts.base > cap * j).astype(jnp.int32)
            i = row + shifts.base - cap * group
            turn = (span - STRIP * group - GHOST) & (span - 1)
            for z in range(planes):
                head = pltpu.roll(shifted[1 + i, z] + second[1 + i, z], turn, 1)
                body = pltpu.roll(shifted[wide + row, z] + second[wide + row, z], GHOST, 1)
                at = pl.ds(row - GHOST + z * nx, nfields, stride=planes * nx)
                rows_out[at, :] = 0.5 * jnp.where(begins, head, body)
        piece_of(step).start()
        return carry

    lax.fori_loop(0, nx // some, put_rows, 0)
    for step in range(nx // some):
        piece_of(step).wait()


def per_device(state, offsets, fraction, speeds, coupling):
    nfields, planes, nx, span = state.shape
    devices = lax.axis_size("az")
    cap = rows_per_block(devices)
    total = nx + 2 * GHOST
    plan = Messages(cap, total)
    count = len(plan.sizes)
    vmem = pl.BlockSpec(memory_space=pltpu.VMEM)
    smem = pl.BlockSpec(memory_space=pltpu.SMEM)
    hbm = pl.BlockSpec(memory_space=pl.ANY)
    *sent, key, weights = pl.pallas_call(
        functools.partial(pack_kernel, cap, nx, planes, devices),
        out_shape=[jax.ShapeDtypeStruct((n, planes, nfields, span), jnp.float32) for n in plan.sizes]
        + [
            jax.ShapeDtypeStruct((1,), jnp.int32),
            jax.ShapeDtypeStruct((9 + nfields, nfields, span), jnp.float32),
        ],
        in_specs=[hbm] * 4,
        out_specs=[vmem] * count + [smem, vmem],
        scratch_shapes=[
            pltpu.SMEM(offsets.shape, jnp.int32),
            pltpu.VMEM(speeds.shape, jnp.float32),
            pltpu.VMEM(coupling.shape, jnp.float32),
            pltpu.VMEM((nfields * planes * nx, span), jnp.float32),
            pltpu.SemaphoreType.DMA((4,)),
        ],
        name="pack",
    )(offsets, speeds, coupling, state.reshape(nfields * planes * nx, span))

    order = [plan.last, plan.last - 1] + list(range(plan.last - 1)) + [plan.last + 1, plan.last + 2]

    def branch(block, moves):
        def send(*parts):
            received = []
            for n in order:
                part, at = parts[n], 0
                pieces = []
                for size, group in moves[n]:
                    steps = (block + group) % devices
                    piece = part[at : at + size]
                    if steps:
                        piece = lax.ppermute(
                            piece, "az", [(i, (i + steps) % devices) for i in range(devices)]
                        )
                    pieces.append(piece)
                    at += size
                received.append(jnp.concatenate(pieces, axis=0) if pieces else part)
            return received

        return send

    branches = [branch(block, moves) for block in range(devices) for moves in plan.moves]
    arrived = lax.switch(key[0], branches, *sent)
    arrived = [arrived[order.index(n)] for n in range(count)]

    rows = cap + 5 + total + 13
    out = pl.pallas_call(
        functools.partial(step_kernel, cap, nx, planes),
        out_shape=jax.ShapeDtypeStruct((nfields * planes, nx, span), jnp.float32),
        in_specs=[smem, smem, vmem] + [vmem] * count,
        out_specs=hbm,
        scratch_shapes=[pltpu.VMEM((rows, planes, nfields, span), jnp.float32)] * 3
        + [
            pltpu.VMEM((nfields * planes * nx, span), jnp.float32),
            pltpu.SemaphoreType.DMA((nx // OUT_ROWS,)),
        ],
        name="step",
    )(offsets, fraction, weights, *arrived)
    return out.reshape(state.shape)


def solution(mesh):
    return jax.shard_map(
        per_device,
        mesh=mesh,
        in_specs=(P(None, "runs", None, "az"), P("runs"), P("runs"), P(), P()),
        out_specs=P(None, "runs", None, "az"),
        check_vma=False,
    )
```

```python
import functools

import jax
import jax.numpy as jnp
from jax import lax
from jax.experimental import pallas as pl
from jax.experimental.pallas import tpu as pltpu
from jax.sharding import PartitionSpec as P

courant = 0.3
GHOST = 4
EDGE = 2 * GHOST + 1
OUT_ROWS = 16
STRIP = 4 * GHOST


def rows_per_block(devices):
    return 9 if devices <= 16 else 6


class Shifts:
    def __init__(self, offs, cap, span):
        self.offs, self.cap, self.span = offs, cap, span
        start = self.within(0)
        late = [(self.within(m) < start).astype(jnp.int32) for m in range(1, cap)]
        self.base = functools.reduce(lambda a, b: a + b, late) + 1

    def within(self, x):
        return (self.offs[x] + (self.span - GHOST)) & (self.span - 1)

    def of_slot(self, i):
        return self.within(jnp.where(i < self.base, i + self.cap, i) - self.base)


def paired(low, high, together):
    rows, left = [], list(range(high, low - 1, -1))
    while left:
        i = left.pop(0)
        other = together - i
        if other in left:
            left.remove(other)
            rows.append((i, other))
        else:
            rows.append((i, None))
    return rows


class Messages:
    def __init__(self, cap, total):
        few = total % cap
        self.last = total // cap + 1
        self.begin = paired(1, cap, cap + 3)
        self.end = paired(1, cap - 1, cap)
        self.first = paired(cap - few + 1, cap, 2 * cap - few + 1)
        self.over = paired(1, few - 1, few)
        self.few = few
        self.sizes = [cap + 1] * self.last + [
            len(self.begin),
            1 + len(self.end),
            len(self.first) + 1 + len(self.over),
        ]
        full = [[(cap + 1, j)] for j in range(1, self.last)]
        pieces = [(len(self.first), 0), (1 + len(self.over), self.last + 1)]
        self.moves = [
            full + [[], [(len(self.begin), 0)], [(1 + len(self.end), self.last)], []],
            full + [[(cap + 1, self.last)], [], [], pieces],
        ]


def step_weights(speeds, coupling, tile):
    nfields = tile[0]
    rows = lax.broadcasted_iota(jnp.int32, (nfields, nfields), 0)
    cols = lax.broadcasted_iota(jnp.int32, (nfields, nfields), 1)

    def spread(picked):
        return jnp.broadcast_to(jnp.sum(picked, axis=1, keepdims=True), tile)

    terms = []
    for axis in range(3):
        speed = spread(jnp.where(rows == cols, speeds[axis : axis + 1, :], 0.0))
        slope_part = jnp.where(
            speed > 0.0, 0.5 * (1.0 - courant * speed), -0.5 * (1.0 + courant * speed)
        )
        scaled = -courant * speed
        terms += [scaled, scaled * slope_part, speed]
    for r in range(nfields):
        mixed = courant * spread(jnp.where((rows - cols) % nfields == r, coupling[...], 0.0))
        terms.append(mixed + 1.0 if r == 0 else mixed)
    return terms


def pack_kernel(cap, nx, planes, devices, *refs):
    operands, refs = refs[:4], refs[4:]
    held, refs, sem = refs[-5:-1], refs[:-5], refs[-1]
    copies = [pltpu.make_async_copy(a, b, sem.at[n]) for n, (a, b) in enumerate(zip(operands, held))]
    for copy in copies:
        copy.start()
    offs, speeds, coupling, cells = held
    sent, (key, weights) = refs[:-2], refs[-2:]
    nfields, span = sent[0].shape[2:]
    plan = Messages(cap, nx + 2 * GHOST)
    full, (begin, end, rest) = sent[:-3], sent[-3:]
    last, split = plan.last, len(plan.first)
    tile = (nfields, span)
    copies[0].wait()
    shifts = Shifts(offs, cap, span)
    block = ((offs[0] + (devices * span - GHOST)) >> (span.bit_length() - 1)) & (devices - 1)
    key[0] = 2 * block + (shifts.base >= cap + 1 - plan.few).astype(jnp.int32)
    copies[1].wait()
    copies[2].wait()
    for t, term in enumerate(step_weights(speeds, coupling, tile)):
        weights[t] = term
    lane = lax.broadcasted_iota(jnp.int32, tile, 1)
    copies[3].wait()

    def row(i, k, z):
        x = cap * k + i - shifts.base
        source = jnp.where(x < GHOST, x + nx, x) - GHOST
        source = jnp.where(source >= nx, source - nx, source)
        return cells[pl.ds(jnp.clip(source, 0, nx - 1) + z * nx, nfields, stride=planes * nx), :]

    def one_slot(i, carry):
        edges, nearer = carry
        within = shifts.of_slot(i)
        near = lane >= within
        offset = lane - EDGE * (i - 1)
        member = (offset >= 0) & (offset < EDGE)
        nearer = jnp.where(member, (offset + (span - EDGE) >= within).astype(jnp.int32), nearer)
        new = []
        for z in range(planes):
            before = None
            for k in range(last + 1):
                rows = row(i, k, z)
                value = pltpu.roll(rows, within, 1)
                if k:
                    full[k - 1][i, z] = jnp.where(near, value, before)
                piece = pltpu.roll(rows, (within + EDGE * i) & (span - 1), 1)
                new.append(jnp.where(member, piece, edges[z * (last + 1) + k]))
                before = value
        return tuple(new), nearer

    zero = jnp.zeros(tile, jnp.float32)
    carry = (zero,) * (planes * (last + 1)), jnp.zeros(tile, jnp.int32)
    for i in range(1, cap + 1):
        carry = one_slot(i, carry)
    edges, nearer = carry[0], carry[1] > 0
    for z in range(planes):
        for ref, pairs, k, at, below in (
            (begin, plan.begin, 0, 0, False),
            (end, plan.end, last - 1, 1, True),
            (rest, plan.first, 0, 0, False),
            (rest, plan.over, last, split + 1, True),
        ):
            for n, (i, other) in enumerate(pairs):
                within = shifts.of_slot(i)
                value = pltpu.roll(row(i, k, z), within, 1)
                if other is not None:
                    used = lane < within if below else lane >= within
                    value = jnp.where(used, value, row(other, k, z))
                ref[at + n, z] = value
        for j in range(1, last + 2):
            near_edge = edges[z * (last + 1) + j - 1]
            far_edge = edges[z * (last + 1) + max(j - 2, 0)]
            ends = jnp.where(nearer, near_edge, far_edge)
            if j <= last:
                full[j - 1][0, z] = ends
            if j == last:
                end[0, z] = ends
            if j > last:
                rest[split, z] = ends


def minmod(lower, upper):
    return jnp.maximum(jnp.minimum(upper, 0.0), jnp.minimum(lower, jnp.maximum(upper, 0.0)))


def step_kernel(cap, nx, planes, offs, frac, weights, *refs):
    arrived, (out, shifted, first, second, rows_out, sem) = refs[:-6], refs[-6:]
    nfields, span = arrived[0].shape[2:]
    total = nx + 2 * GHOST
    plan = Messages(cap, total)
    last = plan.last
    full, (begin, end, rest) = arrived[:-3], arrived[-3:]
    split = len(plan.first)
    tile = (nfields, span)
    wide = cap + 5
    shifts = Shifts(offs, cap, span)
    lane = lax.broadcasted_iota(jnp.int32, tile, 1)
    slot = lane // STRIP
    lower_half = lane < span // 2
    first_lane = lane == 0

    terms = [weights[t] for t in range(9 + nfields)]
    sx, tx, ax, sy, ty, ay, sz, tz, az = terms[:9]
    px, py, pz = ax > 0.0, ay > 0.0, az > 0.0
    mix = terms[9:]

    many = shifts.base >= cap + 1 - plan.few

    def place(i, pairs, at):
        row, raw = jnp.int32(0), jnp.int32(0)
        for n, (a, b) in enumerate(pairs):
            row = jnp.where(i == a, at + n, row)
            if b is not None:
                row = jnp.where(i == b, at + n, row)
                raw = jnp.where(i == b, 1, raw)
        return row, raw

    def remap_slot(i):
        within = shifts.of_slot(i)
        near = lane >= within
        nearer = lane >= within + (EDGE * i - span)
        begin_row, begin_raw = place(i, plan.begin, 0)
        many_row, many_raw = place(i, plan.first, 0)
        end_row, end_raw = place(i, plan.end, 1)
        over_row, over_raw = place(i, plan.over, split + 1)
        begin_turn = jnp.where(many, many_raw, begin_raw) * within
        end_turn = jnp.where(many, 0, end_raw) * within
        for z in range(planes):
            strip = None
            mains = [
                pltpu.roll(
                    jnp.where(many, rest[many_row, z], begin[begin_row, z]), begin_turn, 1
                )
            ]
            tails = [None]
            for k in range(1, last):
                mains.append(full[k - 1][i, z])
                tails.append(full[k - 1][0, z])
            mains.append(
                pltpu.roll(jnp.where(many, full[last - 1][i, z], end[end_row, z]), end_turn, 1)
            )
            tails.append(jnp.where(many, full[last - 1][0, z], end[0, z]))
            mains.append(pltpu.roll(rest[over_row, z], over_raw * within, 1))
            tails.append(rest[split, z])
            for k in range(last + 1):
                x = jnp.clip(cap * k + i - shifts.base, -1, total)
                f = frac[jnp.clip(x, 0, total - 1)]
                upper = jnp.where(near, mains[k], mains[k + 1])
                ends = tails[k + 1]
                if k < last:
                    ends = jnp.where(nearer, ends, tails[k + 2])
                edge = pltpu.roll(ends, span - EDGE * i, 1)
                edge_lower = pltpu.roll(ends, span - EDGE * i + 1, 1)
                lower = jnp.where(first_lane, edge_lower, pltpu.roll(upper, 1, 1))
                body = (1.0 - f) * upper + f * lower
                edge = (1.0 - f) * edge + f * edge_lower
                shifted[wide + x, z] = body
                piece = pltpu.roll(
                    jnp.where(lower_half, body, edge), (STRIP * k + STRIP // 2) % span, 1
                )
                strip = piece if k == 0 else jnp.where(slot == k, piece, strip)
            shifted[1 + i, z] = strip

    def remap_slots(step, carry):
        for u in range(3):
            remap_slot(3 * step + u + 1)
        return carry

    lax.fori_loop(0, cap // 3, remap_slots, 0)

    def wrap_strips(ref):
        for z in range(planes):
            for i in range(2):
                ref[i, z] = pltpu.roll(ref[i + cap, z], STRIP, 1)
                ref[2 + cap + i, z] = pltpu.roll(ref[2 + i, z], span - STRIP, 1)

    def state_of(u, before, after):
        return sx * u + tx * minmod(before, after)

    def advance(source, unroll, steps, emit):
        def enter(z):
            u = [source[i, z] for i in range(4)]
            jumps = [u[i + 1] - u[i] for i in range(3)]
            low = state_of(u[1], jumps[0], jumps[1])
            here = state_of(u[2], jumps[1], jumps[2])
            return u[2], u[3], jumps[2], here, here - low

        def body(step, carry):
            for k in range(unroll):
                x = 2 + step * unroll + k
                vertical = []
                for z in range(planes):
                    u = carry[z][0]
                    above, below = carry[(z + 1) % planes][0], carry[(z - 1) % planes][0]
                    vertical.append(sz * u + tz * minmod(u - below, above - u))
                following = []
                for z in range(planes):
                    u, ahead_u, jump, here, behind_face = carry[z]
                    beyond = source[x + 2, z]
                    next_jump = beyond - ahead_u
                    there = state_of(ahead_u, jump, next_jump)
                    face = there - here
                    following.append((ahead_u, beyond, next_jump, there, face))
                    value = mix[0] * u + jnp.where(px, behind_face, face)
                    for r in range(1, nfields):
                        value = value + mix[r] * pltpu.roll(u, r, 0)
                    value = value + jnp.where(
                        pz,
                        vertical[z] - vertical[(z - 1) % planes],
                        vertical[(z + 1) % planes] - vertical[z],
                    )
                    near = [pltpu.roll(u, shift % span, 1) if shift else u for shift in (2, 1, 0, -1, -2)]
                    near = [jnp.where(py, near[j], near[j + 1]) for j in range(4)]
                    steps_y = [near[j + 1] - near[j] for j in range(3)]
                    side = sy * steps_y[1] + ty * (
                        minmod(steps_y[1], steps_y[2]) - minmod(steps_y[0], steps_y[1])
                    )
                    emit(x, z, value + side)
                carry = tuple(following)
            return carry

        lax.fori_loop(0, steps, body, tuple(enter(z) for z in range(planes)))

    def put_first(x, z, value):
        first[x, z] = value

    def put_second(x, z, value):
        second[x, z] = value

    unroll = 17
    steps = -(-(wide + total - 4) // unroll)
    wrap_strips(shifted)
    advance(shifted, unroll, steps, put_first)
    wrap_strips(first)
    advance(first, unroll, steps, put_second)

    begins = lane < STRIP // 2

    by_row = rows_out.reshape(nfields * planes, nx, span)
    some = OUT_ROWS

    def piece_of(step):
        part = pl.ds(pl.multiple_of(some * step, some), some)
        return pltpu.make_async_copy(by_row.at[:, part], out.at[:, part], sem.at[step])

    def put_rows(step, carry):
        for k in range(some):
            row = GHOST + some * step + k
            group = jnp.int32(0)
            for j in range(1, last + 1):
                group = group + (row + shifts.base > cap * j).astype(jnp.int32)
            i = row + shifts.base - cap * group
            turn = (span - STRIP * group - GHOST) & (span - 1)
            for z in range(planes):
                head = pltpu.roll(shifted[1 + i, z] + second[1 + i, z], turn, 1)
                body = pltpu.roll(shifted[wide + row, z] + second[wide + row, z], GHOST, 1)
                at = pl.ds(row - GHOST + z * nx, nfields, stride=planes * nx)
                rows_out[at, :] = 0.5 * jnp.where(begins, head, body)
        piece_of(step).start()
        return carry

    lax.fori_loop(0, nx // some, put_rows, 0)
    for step in range(nx // some):
        piece_of(step).wait()


def per_device(state, offsets, fraction, speeds, coupling):
    nfields, planes, nx, span = state.shape
    devices = lax.axis_size("az")
    cap = rows_per_block(devices)
    total = nx + 2 * GHOST
    plan = Messages(cap, total)
    count = len(plan.sizes)
    vmem = pl.BlockSpec(memory_space=pltpu.VMEM)
    smem = pl.BlockSpec(memory_space=pltpu.SMEM)
    hbm = pl.BlockSpec(memory_space=pl.ANY)
    *sent, key, weights = pl.pallas_call(
        functools.partial(pack_kernel, cap, nx, planes, devices),
        out_shape=[jax.ShapeDtypeStruct((n, planes, nfields, span), jnp.float32) for n in plan.sizes]
        + [
            jax.ShapeDtypeStruct((1,), jnp.int32),
            jax.ShapeDtypeStruct((9 + nfields, nfields, span), jnp.float32),
        ],
        in_specs=[hbm] * 4,
        out_specs=[vmem] * count + [smem, vmem],
        scratch_shapes=[
            pltpu.SMEM(offsets.shape, jnp.int32),
            pltpu.VMEM(speeds.shape, jnp.float32),
            pltpu.VMEM(coupling.shape, jnp.float32),
            pltpu.VMEM((nfields * planes * nx, span), jnp.float32),
            pltpu.SemaphoreType.DMA((4,)),
        ],
        name="pack",
    )(offsets, speeds, coupling, state.reshape(nfields * planes * nx, span))

    order = [plan.last, plan.last - 1] + list(range(plan.last - 1)) + [plan.last + 1, plan.last + 2]

    def branch(block, moves):
        def send(*parts):
            received = []
            for n in order:
                part, at = parts[n], 0
                pieces = []
                for size, group in moves[n]:
                    steps = (block + group) % devices
                    piece = part[at : at + size]
                    if steps:
                        piece = lax.ppermute(
                            piece, "az", [(i, (i + steps) % devices) for i in range(devices)]
                        )
                    pieces.append(piece)
                    at += size
                received.append(jnp.concatenate(pieces, axis=0) if pieces else part)
            return received

        return send

    branches = [branch(block, moves) for block in range(devices) for moves in plan.moves]
    arrived = lax.switch(key[0], branches, *sent)
    arrived = [arrived[order.index(n)] for n in range(count)]

    rows = cap + 5 + total + 13
    out = pl.pallas_call(
        functools.partial(step_kernel, cap, nx, planes),
        out_shape=jax.ShapeDtypeStruct((nfields * planes, nx, span), jnp.float32),
        in_specs=[smem, smem, vmem] + [vmem] * count,
        out_specs=hbm,
        scratch_shapes=[pltpu.VMEM((rows, planes, nfields, span), jnp.float32)] * 3
        + [
            pltpu.VMEM((nfields * planes * nx, span), jnp.float32),
            pltpu.SemaphoreType.DMA((nx // OUT_ROWS,)),
        ],
        name="step",
    )(offsets, fraction, weights, *arrived)
    return out.reshape(state.shape)


def solution(mesh):
    return jax.shard_map(
        per_device,
        mesh=mesh,
        in_specs=(P(None, "runs", None, "az"), P("runs"), P("runs"), P(), P()),
        out_specs=P(None, "runs", None, "az"),
        check_vma=False,
    )
```
